32 devices in a mesh: dp: 16 (over z, y, x), tensor: 2 (over core).
Axes of the slice: x: 2, y: 2, z: 4, core: 2. Of those that a mesh axis runs over, the one named last changes fastest.
Arguments:
- layer_input: bfloat16 [16, 512, 4096], P('dp', 'tensor'), may hold values from -6 to 6
- out_grad: bfloat16 [16, 512, 2048], P('dp', None, 'tensor'), may hold values from -6 to 6
- ssd_output: bfloat16 [16, 512, 2048], P('dp', None, 'tensor'), may hold values from -2100 to 2100
- gate_input: bfloat16 [16, 512, 2048], P('dp', None, 'tensor'), may hold values from -6 to 6
- time_step: float32 [16, 512, 32], P('dp', None, 'tensor'), may hold values from 0.5 to 2
- state_in: bfloat16 [16, 512, 512], P('dp', None, 'tensor'), may hold values from -0.8984375 to 0.8984375
- state_out: bfloat16 [16, 512, 512], P('dp', None, 'tensor'), may hold values from -0.8984375 to 0.8984375
- decay_rate: float32 [32], P('tensor'), may hold values from 0 to 1, as said below
- skip_gain: float32 [32], P('tensor'), may hold values from 0.5 to 2
- norm_gain: bfloat16 [2048], P('tensor'), may hold values from 0.099609375 to 1.8984375
- mixer_projection_weight: bfloat16 [4096, 2048], P('dp', 'tensor'), may hold values from -0.09375 to 0.09375
- down_adapter_matrix: bfloat16 [4096, 32], P('dp'), may hold values from -0.09375 to 0.09375
- adapter_b: bfloat16 [32, 2048], P(None, 'tensor'), may hold values from -0.125 to 0.125
Outputs:
- input_grad: bfloat16 [16, 512, 4096], P('dp', 'tensor')
- adapter_a_grad: float32 [4096, 32], P('dp')
- adapter_b_grad: float32 [32, 2048], P(None, 'tensor')
- gain_grad: float32 [2048], P('tensor')
The draws below stay inside these ranges and needn't reach their ends.
Inputs may be any that keep to these rules, and one draw needn't show every extreme that they name: `decay_rate`: per head.
All inputs are finite; a program needn't handle non-finite values.
Results may differ from the reference program's by a relative error of at most 0.0071.
Values may be sent and summed in bfloat16 or wider, within the bound.
A program may use at most 64 MiB of HBM per device.

```python
import math
import jax
import jax.numpy as jnp
from jax import lax

D = 4096
HEADS_DEV = 16
HEAD = 64
N = 256
R = 32
L = 512
GROUPS = 2
HEADS = 32
INNER_PER_SHARD = 1024
INNER = 2048
BATCH = 16
N_TENSOR = 2


def draw_ssd_output(key, part):
    keys = jax.random.split(key, 4)
    array_shape = (BATCH, L, INNER)
    channel = jnp.arange(INNER, dtype=jnp.float32)
    rising_ramp = jnp.exp(math.log(3.0) * channel / max(INNER - 1, 1))
    column_scale = rising_ramp * jnp.exp(jax.random.uniform(keys[0], (INNER,), minval=0.0, maxval=math.log(10.0)))
    row_scale = jnp.exp(jax.random.uniform(keys[1], (BATCH, L, 1), minval=0.0, maxval=math.log(10.0)))
    values = jnp.clip(jax.random.normal(keys[3], array_shape, jnp.float32), -4.0, 4.0)
    return (values * row_scale * column_scale[None, None, :]).astype(jnp.bfloat16)


def draw_decay_rate(key, part):
    lower_log = math.log(0.25 / L)
    upper_log = math.log(24.0 / L)
    return jnp.exp(jax.random.uniform(key, (HEADS,), minval=lower_log, maxval=upper_log)).astype(jnp.float32)


def strengthened(drawn, stream_key, source, target, blocks, factor):
    def block_of(axis_at):
        return (jnp.arange(drawn.shape[axis_at]) // (drawn.shape[axis_at] // blocks)).reshape((-1,) + (1,) * (drawn.ndim - 1 - axis_at))

    one_side = jax.random.permutation(stream_key, blocks)[block_of(target)]
    other_side = (block_of(target) + blocks // 2) % blocks
    return jnp.where((block_of(source) == one_side) | (block_of(source) == other_side), factor * drawn, drawn)


def level_of(own_key, shape, shards, smallest, largest):
    def one(axis_at, blocks):
        heights = jax.random.uniform(jax.random.fold_in(jax.random.fold_in(own_key, 6), axis_at), (blocks,), jnp.float32, smallest / len(shards), largest / len(shards))
        return jnp.repeat(jnp.exp(heights), shape[axis_at] // blocks).reshape((-1,) + (1,) * (len(shape) - axis_at - 1))

    level = one(*shards[0])
    for cut in shards[1:]:
        level = level * one(*cut)
    return level


def scatter_about(own_key, shape, width, reach, cuts=(), kind=jnp.bfloat16):
    drawn = width * jax.random.normal(own_key, shape, jnp.float32)
    if cuts:
        drawn = drawn * level_of(own_key, shape, cuts, -0.22, 0.18)
    return jnp.clip(drawn, -reach, reach).astype(kind)


def noise_with(key, dims, scale, most, cuts, heavy, kind=jnp.bfloat16):
    array = scale * jax.random.normal(key, dims, jnp.float32)
    if cuts:
        array = array * level_of(key, dims, cuts, -0.22, 0.18)
    return jnp.clip(strengthened(array, jax.random.fold_in(key, 3), *heavy), -most, most).astype(kind)


def setup_inputs(seed: int = 0) -> dict:
    key_list = jax.random.split(jax.random.key(seed), 14)
    return {
        "layer_input": noise_with(key_list[0], (BATCH, L, D), 1.0, 6.0, ((0, 16), (1, 2)), (0, 2, 16, 2.0)),
        "out_grad": scatter_about(key_list[1], (BATCH, L, INNER), 1.0, 6.0, ((0, 16), (2, 2))),
        "ssd_output": draw_ssd_output(jax.random.fold_in(key_list[13], 71), 0),
        "gate_input": scatter_about(key_list[3], (BATCH, L, INNER), 1.0, 6.0, ((0, 16), (2, 2))),
        "time_step": jnp.clip(jnp.exp(math.log(2.0) - 1.3862944 * jax.random.uniform(key_list[4], (BATCH, L, HEADS), jnp.float32) ** level_of(key_list[4], (BATCH, L, HEADS), ((0, 16), (2, 2)), -0.2, 0.2)), 0.5, 2.0),
        "state_in": scatter_about(key_list[5], (BATCH, L, GROUPS * N), 0.15, 0.8984375, ((0, 16), (2, 2))),
        "state_out": scatter_about(key_list[6], (BATCH, L, GROUPS * N), 0.15, 0.8984375, ((0, 16), (2, 2))),
        "decay_rate": draw_decay_rate(jax.random.fold_in(key_list[13], 71), 0),
        "skip_gain": jnp.clip(jnp.exp(math.log(2.0) - 1.3862944 * jax.random.uniform(key_list[8], (HEADS,), jnp.float32) ** level_of(key_list[8], (HEADS,), ((0, 2),), -0.2, 0.2)), 0.5, 2.0),
        "norm_gain": jnp.clip(1.0 + 0.18 * jax.random.normal(key_list[9], (INNER,), jnp.float32), 0.099609375, 1.8984375).astype(jnp.bfloat16),
        "mixer_projection_weight": scatter_about(key_list[10], (D, INNER), D ** -0.5, 0.09375, ((0, 16), (1, 2))),
        "down_adapter_matrix": scatter_about(key_list[11], (D, R), D ** -0.5, 0.09375, ((0, 16),)),
        "adapter_b": scatter_about(key_list[12], (R, INNER), INNER ** -0.5, 0.125, ((1, 2),)),
    }


eps_norm = 1e-05
low_rank_scale = 2.0

def reference(layer_input, out_grad, ssd_output, gate_input, time_step, state_in, state_out, decay_rate, skip_gain, norm_gain, mixer_projection_weight, down_adapter_matrix, adapter_b):
    positions = jnp.arange(L)
    causal = positions[:, None] >= positions[None, :]
    gain_full = norm_gain.astype(jnp.float32)
    group_ids = (jnp.arange(HEADS) // HEADS_DEV).astype(jnp.int32)

    def one_sequence(running, inputs):
        first_factor_sum, second_factor_sum, sum_gain = running
        sequence_input, seq_grad, seq_out, seq_gate, seq_step, seq_in, seq_outmap = inputs
        activation = jax.nn.silu(seq_gate.astype(jnp.float32))
        gated_rows = seq_out.astype(jnp.float32) * activation
        grad_rows = seq_grad.astype(jnp.float32)
        gain_out = gain_full[None, :] * grad_rows
        sum_squares = lax.optimization_barrier(jnp.sum(gated_rows * gated_rows, axis=1))
        cross_sum = lax.optimization_barrier(jnp.sum(gain_out * gated_rows, axis=1))
        inverse_rms = lax.rsqrt(sum_squares / INNER + eps_norm)
        ssd_grad = (inverse_rms[:, None] * gain_out - gated_rows * (inverse_rms ** 3 * cross_sum / INNER)[:, None]) * activation
        gain_part = lax.optimization_barrier(jnp.sum(grad_rows * gated_rows * inverse_rms[:, None], axis=0))
        out_groups = seq_outmap.astype(jnp.float32).reshape(L, GROUPS, N)
        in_groups = seq_in.astype(jnp.float32).reshape(L, GROUPS, N)
        scores = jnp.einsum('sgn,tgn->gst', out_groups, in_groups)
        cumulative = jnp.cumsum(-seq_step * decay_rate[None, :], axis=0)
        head_grads = jnp.transpose(ssd_grad.astype(jnp.bfloat16).reshape(L, HEADS, HEAD), (1, 0, 2))

        def per_head(head_items):
            head_cum, head_grad, group_id = head_items
            decay_gap = head_cum[:, None] - head_cum[None, :]
            mix_weights = (scores[group_id] * jnp.exp(jnp.where(causal, decay_gap, -jnp.inf))).astype(jnp.bfloat16)
            return jnp.dot(mix_weights.T, head_grad, preferred_element_type=jnp.float32)
        state_back = lax.map(per_head, (cumulative.T, head_grads, group_ids))
        mixer_input_gradient = (seq_step[:, :, None] * jnp.transpose(state_back, (1, 0, 2)) + skip_gain[None, :, None] * ssd_grad.reshape(L, HEADS, HEAD)).reshape(L, INNER).astype(jnp.bfloat16)
        input_sum = jnp.zeros((L, D), jnp.float32)
        adapter_sum = jnp.zeros((L, R), jnp.float32)
        for block in range(N_TENSOR):
            leading_column = block * INNER_PER_SHARD
            mixer_input_block = mixer_input_gradient[:, leading_column:leading_column + INNER_PER_SHARD]
            adapter_portion = jnp.dot(mixer_input_block, adapter_b[:, leading_column:leading_column + INNER_PER_SHARD].T, preferred_element_type=jnp.float32)
            adapter_sum = adapter_sum + adapter_portion
            input_portion = jnp.dot(mixer_input_block, mixer_projection_weight[:, leading_column:leading_column + INNER_PER_SHARD].T, preferred_element_type=jnp.float32) + low_rank_scale * jnp.dot(adapter_portion.astype(jnp.bfloat16), down_adapter_matrix.T, preferred_element_type=jnp.float32)
            input_sum = input_sum + lax.optimization_barrier(input_portion.astype(jnp.bfloat16)).astype(jnp.float32)
        adapter_token_rows = adapter_sum.astype(jnp.bfloat16)
        first_factor_sum = first_factor_sum + low_rank_scale * jnp.dot(sequence_input.T, adapter_token_rows, preferred_element_type=jnp.float32)
        adapter_input_rows = jnp.dot(sequence_input, down_adapter_matrix, preferred_element_type=jnp.float32).astype(jnp.bfloat16)
        second_factor_sum = second_factor_sum + low_rank_scale * jnp.dot(adapter_input_rows.T, mixer_input_gradient, preferred_element_type=jnp.float32)
        sum_gain = sum_gain + gain_part
        return ((first_factor_sum, second_factor_sum, sum_gain), input_sum.astype(jnp.bfloat16))
    start_sums = (jnp.zeros((D, R), jnp.float32), jnp.zeros((R, INNER), jnp.float32), jnp.zeros((INNER,), jnp.float32))
    final_sums, input_grad = lax.scan(one_sequence, start_sums, (layer_input, out_grad, ssd_output, gate_input, time_step, state_in, state_out))
    grad_scale = float(BATCH * L) ** (-0.5)
    return (input_grad, final_sums[0] * grad_scale, final_sums[1] * grad_scale, final_sums[2] * grad_scale)
```

```python
import functools

import jax
import jax.numpy as jnp
from jax import lax
from jax.experimental import pallas as pl
from jax.experimental.pallas import tpu as pltpu
from jax.sharding import PartitionSpec as P

eps_norm = 1e-05
low_rank_scale = 2.0
MESH = pl.DeviceIdType.MESH


def loop(count, step):
    def run(i, carry):
        step(i)
        return carry

    lax.fori_loop(0, count, run, 0)


def greet_kernel_peers(axis_counts):
    barrier = pltpu.get_barrier_semaphore()
    for axis, count in axis_counts:
        me = lax.axis_index(axis)
        loop(
            count - 1,
            lambda i, axis=axis, me=me, count=count: pl.semaphore_signal(
                barrier, inc=1, device_id={axis: lax.rem(me + 1 + i, count)}, device_id_type=MESH
            ),
        )
    pl.semaphore_wait(barrier, sum(count - 1 for _, count in axis_counts))


def exchange(axis, count, source, landing, send_sem, recv_sem):
    me = lax.axis_index(axis)

    def copy(peer, slot):
        return pltpu.make_async_remote_copy(
            src_ref=source(peer),
            dst_ref=landing.at[slot],
            send_sem=send_sem.at[peer],
            recv_sem=recv_sem.at[slot],
            device_id={axis: peer},
            device_id_type=MESH,
        )

    def start(i):
        copy(lax.rem(me + 1 + i, count), me).start()

    def finish(i):
        peer = lax.rem(me + 1 + i, count)
        copy(peer, peer).wait_send()
        copy(peer, peer).wait_recv()

    return lambda: loop(count - 1, start), lambda: loop(count - 1, finish)


def gather_kernel(count, own_ref, out_ref, landing, send_sem, recv_sem):
    me = lax.axis_index("dp")
    greet_kernel_peers((("dp", count),))
    start, finish = exchange("dp", count, lambda peer: own_ref, landing, send_sem, recv_sem)
    start()
    landing[me] = own_ref[...]
    finish()
    out_ref[...] = landing[...]


def gather_rows(own, count):
    shape = (count,) + own.shape
    return pl.pallas_call(
        functools.partial(gather_kernel, count),
        out_shape=jax.ShapeDtypeStruct(shape, own.dtype),
        in_specs=[pl.BlockSpec(memory_space=pltpu.VMEM)],
        out_specs=pl.BlockSpec(memory_space=pltpu.VMEM),
        scratch_shapes=[
            pltpu.VMEM(shape, own.dtype),
            pltpu.SemaphoreType.DMA((count,)),
            pltpu.SemaphoreType.DMA((count,)),
        ],
        compiler_params=pltpu.CompilerParams(
            collective_id=0, has_side_effects=True, vmem_limit_bytes=16 * 2**20
        ),
    )(own)


def reduce_kernel(
    count, tensors, scale, a_ref, b_ref, a_out, b_out,
    a_land, b_land, a_pair, b_back, a_part, b_part,
    a_send, a_recv, b_send, b_recv, p_send, p_recv, r_send, r_recv,
):
    me = lax.axis_index("dp")
    pair_me = lax.axis_index("tensor")
    greet_kernel_peers((("dp", count), ("tensor", tensors)))
    b_start, b_finish = exchange("dp", count, lambda p: b_ref.at[p], b_land, b_send, b_recv)
    a_start, a_finish = exchange("dp", count, lambda p: a_ref.at[p], a_land, a_send, a_recv)
    r_start, r_finish = exchange("dp", count, lambda p: b_part, b_back, r_send, r_recv)
    p_start, p_finish = exchange("tensor", tensors, lambda p: a_part, a_pair, p_send, p_recv)
    b_start()
    a_start()

    b_part[...] = b_ref[me]
    a_part[...] = a_ref[me]
    b_finish()

    def add_b(i):
        b_part[...] += b_land[lax.rem(me + 1 + i, count)]

    loop(count - 1, add_b)
    b_part[...] *= scale
    r_start()
    b_back[me] = b_part[...]
    a_finish()

    def add_a(i):
        a_part[...] += a_land[lax.rem(me + 1 + i, count)]

    loop(count - 1, add_a)
    p_start()
    a_pair[pair_me] = a_part[...]
    p_finish()
    total = a_pair[0]
    for k in range(1, tensors):
        total = total + a_pair[k]
    a_out[...] = total * scale
    r_finish()
    b_out[...] = b_back[...]


def reduce_all(a_parts, b_parts, tensors, scale):
    count = a_parts.shape[0]
    f32 = jnp.float32
    return pl.pallas_call(
        functools.partial(reduce_kernel, count, tensors, scale),
        out_shape=(
            jax.ShapeDtypeStruct(a_parts.shape[1:], f32),
            jax.ShapeDtypeStruct(b_parts.shape, f32),
        ),
        in_specs=[pl.BlockSpec(memory_space=pltpu.VMEM)] * 2,
        out_specs=(pl.BlockSpec(memory_space=pltpu.VMEM),) * 2,
        scratch_shapes=[
            pltpu.VMEM(a_parts.shape, f32),
            pltpu.VMEM(b_parts.shape, f32),
            pltpu.VMEM((tensors,) + a_parts.shape[1:], f32),
            pltpu.VMEM(b_parts.shape, f32),
            pltpu.VMEM(a_parts.shape[1:], f32),
            pltpu.VMEM(b_parts.shape[1:], f32),
        ]
        + [pltpu.SemaphoreType.DMA((count,))] * 4
        + [pltpu.SemaphoreType.DMA((tensors,))] * 2
        + [pltpu.SemaphoreType.DMA((count,))] * 2,
        compiler_params=pltpu.CompilerParams(
            collective_id=1, has_side_effects=True, vmem_limit_bytes=16 * 2**20
        ),
    )(a_parts, b_parts)


def body(
    layer_input,
    out_grad,
    ssd_output,
    gate_input,
    time_step,
    state_in,
    state_out,
    decay_rate,
    skip_gain,
    norm_gain,
    mixer_projection_weight,
    down_adapter_matrix,
    adapter_b,
):
    tensor_count = lax.axis_size("tensor")
    data_count = lax.axis_size("dp")
    seq_len = out_grad.shape[1]
    inner_dev = out_grad.shape[2]
    heads_dev = time_step.shape[2]
    head_size = inner_dev // heads_dev
    row_count = layer_input.shape[1]
    shard_rows = down_adapter_matrix.shape[0]
    inner_all = inner_dev * tensor_count
    grad_scale = float(data_count * seq_len) ** (-0.5)
    activation = jax.nn.silu(gate_input[0].astype(jnp.float32))
    gated_rows = ssd_output[0].astype(jnp.float32) * activation
    grad_rows = out_grad[0].astype(jnp.float32)
    gain_out = norm_gain.astype(jnp.float32)[None, :] * grad_rows
    sum_squares, cross_sum = lax.psum(
        (jnp.sum(gated_rows * gated_rows, axis=1), jnp.sum(gain_out * gated_rows, axis=1)), "tensor"
    )
    inverse_rms = lax.rsqrt(sum_squares / inner_all + eps_norm)
    ssd_grad = (
        inverse_rms[:, None] * gain_out
        - gated_rows * (inverse_rms**3 * cross_sum / inner_all)[:, None]
    ) * activation
    gain_part = jnp.sum(grad_rows * gated_rows * inverse_rms[:, None], axis=0)
    scores = lax.dot_general(
        state_out[0], state_in[0], (((1,), (1,)), ((), ())), preferred_element_type=jnp.float32
    )
    cumulative = jnp.cumsum(-time_step[0] * decay_rate[None, :], axis=0)
    positions = jnp.arange(seq_len)
    causal = positions[:, None] >= positions[None, :]
    head_grads = jnp.transpose(
        ssd_grad.astype(jnp.bfloat16).reshape(seq_len, heads_dev, head_size), (1, 0, 2)
    )

    def per_head(head_items):
        head_cum, head_grad = head_items
        decay_gap = head_cum[:, None] - head_cum[None, :]
        mix_weights = (scores * jnp.exp(jnp.where(causal, decay_gap, -jnp.inf))).astype(
            jnp.bfloat16
        )
        return lax.dot_general(
            mix_weights, head_grad, (((0,), (0,)), ((), ())), preferred_element_type=jnp.float32
        )

    state_back = lax.map(per_head, (cumulative.T, head_grads))
    mixer_input_gradient = (
        (
            time_step[0][:, :, None] * jnp.transpose(state_back, (1, 0, 2))
            + skip_gain[None, :, None] * ssd_grad.reshape(seq_len, heads_dev, head_size)
        )
        .reshape(seq_len, inner_dev)
        .astype(jnp.bfloat16)
    )
    adapter_portion = lax.dot_general(
        mixer_input_gradient,
        adapter_b,
        (((1,), (1,)), ((), ())),
        preferred_element_type=jnp.float32,
    )
    adapter_total = lax.psum(adapter_portion, "tensor")
    own_rows = lax.dynamic_slice_in_dim(
        adapter_total, lax.axis_index("tensor") * row_count, row_count, 0
    ).astype(jnp.bfloat16)
    adapter_bf = adapter_portion.astype(jnp.bfloat16)
    sequence_input = layer_input[0]
    rank = down_adapter_matrix.shape[1]
    panel_rows = lax.all_gather(mixer_projection_weight, "dp", axis=0, tiled=True)
    factor_cols = (
        gather_rows(down_adapter_matrix.T, data_count).transpose(1, 0, 2).reshape(rank, -1)
    )
    first_factor_partial = low_rank_scale * lax.dot_general(
        own_rows, sequence_input, (((0,), (0,)), ((), ())), preferred_element_type=jnp.float32
    )
    a_parts = first_factor_partial.reshape(rank, data_count, shard_rows).transpose(1, 0, 2)
    adapter_input_rows = lax.dot_general(
        sequence_input, factor_cols, (((1,), (1,)), ((), ())), preferred_element_type=jnp.float32
    )
    adapter_full = lax.all_gather(
        adapter_input_rows.astype(jnp.bfloat16), "tensor", axis=0, tiled=True
    )
    second_factor_partial = low_rank_scale * lax.dot_general(
        adapter_full,
        mixer_input_gradient,
        (((0,), (0,)), ((), ())),
        preferred_element_type=jnp.float32,
    )
    b_words = (rank + 1) * inner_dev
    chunk_rows = -(-b_words // (data_count * 1024)) * 8
    b_parts = jnp.concatenate(
        [
            second_factor_partial.reshape(-1, 128),
            gain_part.reshape(-1, 128),
            jnp.zeros((data_count * chunk_rows - b_words // 128, 128), jnp.float32),
        ]
    ).reshape(data_count, chunk_rows, 128)
    a_total, b_total = reduce_all(a_parts, b_parts, tensor_count, grad_scale)
    b_lines = b_total.reshape(-1, 128)
    b_count = rank * inner_dev // 128
    adapter_b_grad = b_lines[:b_count].reshape(rank, inner_dev)
    gain_grad = b_lines[b_count : b_words // 128].reshape(inner_dev)
    block = lax.dot_general(
        mixer_input_gradient,
        panel_rows,
        (((1,), (1,)), ((), ())),
        preferred_element_type=jnp.float32,
    ) + low_rank_scale * jnp.dot(adapter_bf, factor_cols, preferred_element_type=jnp.float32)
    input_grad = lax.psum_scatter(
        block.astype(jnp.bfloat16), "tensor", scatter_dimension=0, tiled=True
    )[None]
    return (input_grad, a_total.T, adapter_b_grad, gain_grad)


def solution(mesh):
    return jax.shard_map(
        body,
        mesh=mesh,
        in_specs=(
            P("dp", "tensor", None),
            P("dp", None, "tensor"),
            P("dp", None, "tensor"),
            P("dp", None, "tensor"),
            P("dp", None, "tensor"),
            P("dp", None, "tensor"),
            P("dp", None, "tensor"),
            P("tensor"),
            P("tensor"),
            P("tensor"),
            P("dp", "tensor"),
            P("dp", None),
            P(None, "tensor"),
        ),
        out_specs=(P("dp", "tensor", None), P("dp", None), P(None, "tensor"), P("tensor")),
        check_vma=False,
    )
```

```python
import functools

import jax
import jax.numpy as jnp
from jax import lax
from jax.experimental import pallas as pl
from jax.experimental.pallas import tpu as pltpu
from jax.sharding import PartitionSpec as P

eps_norm = 1e-05
low_rank_scale = 2.0
MESH = pl.DeviceIdType.MESH


def loop(count, step):
    def run(i, carry):
        step(i)
        return carry

    lax.fori_loop(0, count, run, 0)


def greet_kernel_peers(axis_counts):
    barrier = pltpu.get_barrier_semaphore()
    for axis, count in axis_counts:
        me = lax.axis_index(axis)
        loop(
            count - 1,
            lambda i, axis=axis, me=me, count=count: pl.semaphore_signal(
                barrier, inc=1, device_id={axis: lax.rem(me + 1 + i, count)}, device_id_type=MESH
            ),
        )
    pl.semaphore_wait(barrier, sum(count - 1 for _, count in axis_counts))


def exchange(axis, count, source, landing, send_sem, recv_sem):
    me = lax.axis_index(axis)

    def copy(peer, slot):
        return pltpu.make_async_remote_copy(
            src_ref=source(peer),
            dst_ref=landing.at[slot],
            send_sem=send_sem.at[peer],
            recv_sem=recv_sem.at[slot],
            device_id={axis: peer},
            device_id_type=MESH,
        )

    def start(i):
        copy(lax.rem(me + 1 + i, count), me).start()

    def finish(i):
        peer = lax.rem(me + 1 + i, count)
        copy(peer, peer).wait_send()
        copy(peer, peer).wait_recv()

    return lambda: loop(count - 1, start), lambda: loop(count - 1, finish)


def gather_kernel(count, own_ref, out_ref, landing, send_sem, recv_sem):
    me = lax.axis_index("dp")
    greet_kernel_peers((("dp", count),))
    start, finish = exchange("dp", count, lambda peer: own_ref, landing, send_sem, recv_sem)
    start()
    landing[me] = own_ref[...]
    finish()
    out_ref[...] = landing[...]


def gather_rows(own, count):
    shape = (count,) + own.shape
    return pl.pallas_call(
        functools.partial(gather_kernel, count),
        out_shape=jax.ShapeDtypeStruct(shape, own.dtype),
        in_specs=[pl.BlockSpec(memory_space=pltpu.VMEM)],
        out_specs=pl.BlockSpec(memory_space=pltpu.VMEM),
        scratch_shapes=[
            pltpu.VMEM(shape, own.dtype),
            pltpu.SemaphoreType.DMA((count,)),
            pltpu.SemaphoreType.DMA((count,)),
        ],
        compiler_params=pltpu.CompilerParams(
            collective_id=0, has_side_effects=True, vmem_limit_bytes=16 * 2**20
        ),
    )(own)


def reduce_kernel(
    count, tensors, scale, a_ref, b_ref, a_out, b_out,
    a_land, b_land, a_pair, b_back, a_part, b_part,
    a_send, a_recv, b_send, b_recv, p_send, p_recv, r_send, r_recv,
):
    me = lax.axis_index("dp")
    pair_me = lax.axis_index("tensor")
    greet_kernel_peers((("dp", count), ("tensor", tensors)))
    b_start, b_finish = exchange("dp", count, lambda p: b_ref.at[p], b_land, b_send, b_recv)
    a_start, a_finish = exchange("dp", count, lambda p: a_ref.at[p], a_land, a_send, a_recv)
    r_start, r_finish = exchange("dp", count, lambda p: b_part, b_back, r_send, r_recv)
    p_start, p_finish = exchange("tensor", tensors, lambda p: a_part, a_pair, p_send, p_recv)
    b_start()
    a_start()

    b_part[...] = b_ref[me]
    a_part[...] = a_ref[me]
    b_finish()

    def add_b(i):
        b_part[...] += b_land[lax.rem(me + 1 + i, count)]

    loop(count - 1, add_b)
    b_part[...] *= scale
    r_start()
    b_back[me] = b_part[...]
    a_finish()

    def add_a(i):
        a_part[...] += a_land[lax.rem(me + 1 + i, count)]

    loop(count - 1, add_a)
    p_start()
    a_pair[pair_me] = a_part[...]
    p_finish()
    total = a_pair[0]
    for k in range(1, tensors):
        total = total + a_pair[k]
    a_out[...] = total * scale
    r_finish()
    b_out[...] = b_back[...]


def reduce_all(a_parts, b_parts, tensors, scale):
    count = a_parts.shape[0]
    f32 = jnp.float32
    return pl.pallas_call(
        functools.partial(reduce_kernel, count, tensors, scale),
        out_shape=(
            jax.ShapeDtypeStruct(a_parts.shape[1:], f32),
            jax.ShapeDtypeStruct(b_parts.shape, f32),
        ),
        in_specs=[pl.BlockSpec(memory_space=pltpu.VMEM)] * 2,
        out_specs=(pl.BlockSpec(memory_space=pltpu.VMEM),) * 2,
        scratch_shapes=[
            pltpu.VMEM(a_parts.shape, f32),
            pltpu.VMEM(b_parts.shape, f32),
            pltpu.VMEM((tensors,) + a_parts.shape[1:], f32),
            pltpu.VMEM(b_parts.shape, f32),
            pltpu.VMEM(a_parts.shape[1:], f32),
            pltpu.VMEM(b_parts.shape[1:], f32),
        ]
        + [pltpu.SemaphoreType.DMA((count,))] * 4
        + [pltpu.SemaphoreType.DMA((tensors,))] * 2
        + [pltpu.SemaphoreType.DMA((count,))] * 2,
        compiler_params=pltpu.CompilerParams(
            collective_id=1, has_side_effects=True, vmem_limit_bytes=16 * 2**20
        ),
    )(a_parts, b_parts)


def body(
    layer_input,
    out_grad,
    ssd_output,
    gate_input,
    time_step,
    state_in,
    state_out,
    decay_rate,
    skip_gain,
    norm_gain,
    mixer_projection_weight,
    down_adapter_matrix,
    adapter_b,
):
    tensor_count = lax.axis_size("tensor")
    data_count = lax.axis_size("dp")
    seq_len = out_grad.shape[1]
    inner_dev = out_grad.shape[2]
    heads_dev = time_step.shape[2]
    head_size = inner_dev // heads_dev
    row_count = layer_input.shape[1]
    shard_rows = down_adapter_matrix.shape[0]
    inner_all = inner_dev * tensor_count
    grad_scale = float(data_count * seq_len) ** (-0.5)
    activation = jax.nn.silu(gate_input[0].astype(jnp.float32))
    gated_rows = ssd_output[0].astype(jnp.float32) * activation
    grad_rows = out_grad[0].astype(jnp.float32)
    gain_out = norm_gain.astype(jnp.float32)[None, :] * grad_rows
    sum_squares, cross_sum = lax.psum(
        jnp.stack(
            [jnp.sum(gated_rows * gated_rows, axis=1), jnp.sum(gain_out * gated_rows, axis=1)]
        ),
        "tensor",
    )
    inverse_rms = lax.rsqrt(sum_squares / inner_all + eps_norm)
    ssd_grad = (
        inverse_rms[:, None] * gain_out
        - gated_rows * (inverse_rms**3 * cross_sum / inner_all)[:, None]
    ) * activation
    gain_part = jnp.sum(grad_rows * gated_rows * inverse_rms[:, None], axis=0)
    scores = lax.dot_general(
        state_out[0], state_in[0], (((1,), (1,)), ((), ())), preferred_element_type=jnp.float32
    )
    cumulative = jnp.cumsum(-time_step[0] * decay_rate[None, :], axis=0)
    positions = jnp.arange(seq_len)
    causal = positions[:, None] >= positions[None, :]
    head_grads = jnp.transpose(
        ssd_grad.astype(jnp.bfloat16).reshape(seq_len, heads_dev, head_size), (1, 0, 2)
    )

    def per_head(head_items):
        head_cum, head_grad = head_items
        decay_gap = head_cum[:, None] - head_cum[None, :]
        mix_weights = (scores * jnp.exp(jnp.where(causal, decay_gap, -jnp.inf))).astype(
            jnp.bfloat16
        )
        return lax.dot_general(
            mix_weights, head_grad, (((0,), (0,)), ((), ())), preferred_element_type=jnp.float32
        )

    state_back = lax.map(per_head, (cumulative.T, head_grads))
    mixer_input_gradient = (
        (
            time_step[0][:, :, None] * jnp.transpose(state_back, (1, 0, 2))
            + skip_gain[None, :, None] * ssd_grad.reshape(seq_len, heads_dev, head_size)
        )
        .reshape(seq_len, inner_dev)
        .astype(jnp.bfloat16)
    )
    adapter_portion = lax.dot_general(
        mixer_input_gradient,
        adapter_b,
        (((1,), (1,)), ((), ())),
        preferred_element_type=jnp.float32,
    )
    adapter_total = lax.psum(adapter_portion, "tensor")
    own_rows = lax.dynamic_slice_in_dim(
        adapter_total, lax.axis_index("tensor") * row_count, row_count, 0
    ).astype(jnp.bfloat16)
    adapter_bf = adapter_portion.astype(jnp.bfloat16)
    sequence_input = layer_input[0]
    rank = down_adapter_matrix.shape[1]
    panel_rows = lax.all_gather(mixer_projection_weight, "dp", axis=0, tiled=True)
    factor_cols = (
        gather_rows(down_adapter_matrix.T, data_count).transpose(1, 0, 2).reshape(rank, -1)
    )
    first_factor_partial = low_rank_scale * lax.dot_general(
        own_rows, sequence_input, (((0,), (0,)), ((), ())), preferred_element_type=jnp.float32
    )
    a_parts = first_factor_partial.reshape(rank, data_count, shard_rows).transpose(1, 0, 2)
    adapter_input_rows = lax.dot_general(
        sequence_input, factor_cols, (((1,), (1,)), ((), ())), preferred_element_type=jnp.float32
    )
    adapter_full = lax.all_gather(
        adapter_input_rows.astype(jnp.bfloat16), "tensor", axis=0, tiled=True
    )
    second_factor_partial = low_rank_scale * lax.dot_general(
        adapter_full,
        mixer_input_gradient,
        (((0,), (0,)), ((), ())),
        preferred_element_type=jnp.float32,
    )
    b_words = (rank + 1) * inner_dev
    chunk_rows = -(-b_words // (data_count * 1024)) * 8
    b_parts = jnp.concatenate(
        [
            second_factor_partial.reshape(-1, 128),
            gain_part.reshape(-1, 128),
            jnp.zeros((data_count * chunk_rows - b_words // 128, 128), jnp.float32),
        ]
    ).reshape(data_count, chunk_rows, 128)
    a_total, b_total = reduce_all(a_parts, b_parts, tensor_count, grad_scale)
    panel_rows, a_total, b_total = lax.optimization_barrier((panel_rows, a_total, b_total))
    b_lines = b_total.reshape(-1, 128)
    b_count = rank * inner_dev // 128
    adapter_b_grad = b_lines[:b_count].reshape(rank, inner_dev)
    gain_grad = b_lines[b_count : b_words // 128].reshape(inner_dev)
    block = lax.dot_general(
        mixer_input_gradient,
        panel_rows,
        (((1,), (1,)), ((), ())),
        preferred_element_type=jnp.float32,
    ) + low_rank_scale * jnp.dot(adapter_bf, factor_cols, preferred_element_type=jnp.float32)
    input_grad = lax.psum_scatter(
        block.astype(jnp.bfloat16), "tensor", scatter_dimension=0, tiled=True
    )[None]
    return (input_grad, a_total.T, adapter_b_grad, gain_grad)


def solution(mesh):
    return jax.shard_map(
        body,
        mesh=mesh,
        in_specs=(
            P("dp", "tensor", None),
            P("dp", None, "tensor"),
            P("dp", None, "tensor"),
            P("dp", None, "tensor"),
            P("dp", None, "tensor"),
            P("dp", None, "tensor"),
            P("dp", None, "tensor"),
            P("tensor"),
            P("tensor"),
            P("tensor"),
            P("dp", "tensor"),
            P("dp", None),
            P(None, "tensor"),
        ),
        out_specs=(P("dp", "tensor", None), P("dp", None), P(None, "tensor"), P("tensor")),
        check_vma=False,
    )
```

```python
import functools

import jax
import jax.numpy as jnp
from jax import lax
from jax.experimental import pallas as pl
from jax.experimental.pallas import tpu as pltpu
from jax.sharding import PartitionSpec as P

eps_norm = 1e-05
low_rank_scale = 2.0
MESH = pl.DeviceIdType.MESH


def loop(count, step):
    def run(i, carry):
        step(i)
        return carry

    lax.fori_loop(0, count, run, 0)


def greet_kernel_peers(axis_counts):
    barrier = pltpu.get_barrier_semaphore()
    for axis, count in axis_counts:
        me = lax.axis_index(axis)
        loop(
            count - 1,
            lambda i, axis=axis, me=me, count=count: pl.semaphore_signal(
                barrier, inc=1, device_id={axis: lax.rem(me + 1 + i, count)}, device_id_type=MESH
            ),
        )
    pl.semaphore_wait(barrier, sum(count - 1 for _, count in axis_counts))


def exchange(axis, count, source, landing, send_sem, recv_sem):
    me = lax.axis_index(axis)

    def copy(peer, slot):
        return pltpu.make_async_remote_copy(
            src_ref=source(peer),
            dst_ref=landing.at[slot],
            send_sem=send_sem.at[peer],
            recv_sem=recv_sem.at[slot],
            device_id={axis: peer},
            device_id_type=MESH,
        )

    def start(i):
        copy(lax.rem(me + 1 + i, count), me).start()

    def finish(i):
        peer = lax.rem(me + 1 + i, count)
        copy(peer, peer).wait_send()
        copy(peer, peer).wait_recv()

    return lambda: loop(count - 1, start), lambda: loop(count - 1, finish)


def gather_kernel(count, own_ref, out_ref, landing, send_sem, recv_sem):
    me = lax.axis_index("dp")
    greet_kernel_peers((("dp", count),))
    start, finish = exchange("dp", count, lambda peer: own_ref, landing, send_sem, recv_sem)
    start()
    landing[me] = own_ref[...]
    finish()
    out_ref[...] = landing[...]


def gather_rows(own, count):
    shape = (count,) + own.shape
    return pl.pallas_call(
        functools.partial(gather_kernel, count),
        out_shape=jax.ShapeDtypeStruct(shape, own.dtype),
        in_specs=[pl.BlockSpec(memory_space=pltpu.VMEM)],
        out_specs=pl.BlockSpec(memory_space=pltpu.VMEM),
        scratch_shapes=[
            pltpu.VMEM(shape, own.dtype),
            pltpu.SemaphoreType.DMA((count,)),
            pltpu.SemaphoreType.DMA((count,)),
        ],
        compiler_params=pltpu.CompilerParams(
            collective_id=0, has_side_effects=True, vmem_limit_bytes=16 * 2**20
        ),
    )(own)


def reduce_kernel(
    count, tensors, scale, a_ref, b_ref, a_out, b_out,
    a_land, b_land, a_pair, b_back, a_part, b_part,
    a_send, a_recv, b_send, b_recv, p_send, p_recv, r_send, r_recv,
):
    me = lax.axis_index("dp")
    pair_me = lax.axis_index("tensor")
    greet_kernel_peers((("dp", count), ("tensor", tensors)))
    b_start, b_finish = exchange("dp", count, lambda p: b_ref.at[p], b_land, b_send, b_recv)
    a_start, a_finish = exchange("dp", count, lambda p: a_ref.at[p], a_land, a_send, a_recv)
    r_start, r_finish = exchange("dp", count, lambda p: b_part, b_back, r_send, r_recv)
    p_start, p_finish = exchange("tensor", tensors, lambda p: a_part, a_pair, p_send, p_recv)
    b_start()
    a_start()

    b_part[...] = b_ref[me].astype(jnp.float32)
    a_part[...] = a_ref[me].astype(jnp.float32)
    b_finish()

    def add_b(i):
        b_part[...] += b_land[lax.rem(me + 1 + i, count)].astype(jnp.float32)

    loop(count - 1, add_b)
    b_part[...] *= scale
    r_start()
    b_back[me] = b_part[...]
    a_finish()

    def add_a(i):
        a_part[...] += a_land[lax.rem(me + 1 + i, count)].astype(jnp.float32)

    loop(count - 1, add_a)
    p_start()
    a_pair[pair_me] = a_part[...]
    p_finish()
    total = a_pair[0]
    for k in range(1, tensors):
        total = total + a_pair[k]
    a_out[...] = total * scale
    r_finish()
    b_out[...] = b_back[...]


def reduce_all(a_parts, b_parts, tensors, scale):
    count = a_parts.shape[0]
    f32 = jnp.float32
    return pl.pallas_call(
        functools.partial(reduce_kernel, count, tensors, scale),
        out_shape=(
            jax.ShapeDtypeStruct(a_parts.shape[1:], f32),
            jax.ShapeDtypeStruct(b_parts.shape, f32),
        ),
        in_specs=[pl.BlockSpec(memory_space=pltpu.VMEM)] * 2,
        out_specs=(pl.BlockSpec(memory_space=pltpu.VMEM),) * 2,
        scratch_shapes=[
            pltpu.VMEM(a_parts.shape, a_parts.dtype),
            pltpu.VMEM(b_parts.shape, b_parts.dtype),
            pltpu.VMEM((tensors,) + a_parts.shape[1:], f32),
            pltpu.VMEM(b_parts.shape, f32),
            pltpu.VMEM(a_parts.shape[1:], f32),
            pltpu.VMEM(b_parts.shape[1:], f32),
        ]
        + [pltpu.SemaphoreType.DMA((count,))] * 4
        + [pltpu.SemaphoreType.DMA((tensors,))] * 2
        + [pltpu.SemaphoreType.DMA((count,))] * 2,
        compiler_params=pltpu.CompilerParams(
            collective_id=1, has_side_effects=True, vmem_limit_bytes=16 * 2**20
        ),
    )(a_parts, b_parts)


def project_kernel(
    tensors, x_ref, panel_hbm, low_ref, factor_ref, out_ref,
    panel, outgoing, landing, panel_sem, send_sem, recv_sem,
):
    me = lax.axis_index("tensor")
    rows = out_ref.shape[0]
    _, tiles, _, tile = landing.shape

    def columns(j):
        return pl.ds(pl.multiple_of(j * tile, tile), tile)

    def fetch(j):
        return pltpu.make_async_copy(
            panel_hbm.at[columns(j)], panel.at[columns(j)], panel_sem.at[j]
        )

    def copy(peer, slot, j):
        return pltpu.make_async_remote_copy(
            src_ref=outgoing.at[peer, j],
            dst_ref=landing.at[slot, j],
            send_sem=send_sem.at[peer, j],
            recv_sem=recv_sem.at[slot, j],
            device_id={"tensor": peer},
            device_id_type=MESH,
        )

    def product(owner, j):
        tokens = pl.ds(pl.multiple_of(owner * rows, rows), rows)
        full = lax.dot_general(
            x_ref[tokens, :], panel[columns(j), :], (((1,), (1,)), ((), ())),
            preferred_element_type=jnp.float32,
        )
        low = jnp.dot(
            low_ref[tokens, :], factor_ref[:, columns(j)], preferred_element_type=jnp.float32
        )
        return (full + low_rank_scale * low).astype(jnp.bfloat16)

    loop(tiles, lambda j: fetch(j).start())
    greet_kernel_peers((("tensor", tensors),))
    for i in range(tensors - 1):
        peer = lax.rem(me + 1 + i, tensors)

        def send(j, i=i, peer=peer):
            if i == 0:
                fetch(j).wait()
            outgoing[peer, j] = product(peer, j)
            copy(peer, me, j).start()

        loop(tiles, send)

    def own(j):
        total = product(me, j).astype(jnp.float32)
        for i in range(tensors - 1):
            peer = lax.rem(me + 1 + i, tensors)
            copy(peer, peer, j).wait_recv()
            total = total + landing[peer, j].astype(jnp.float32)
        out_ref[:, columns(j)] = total.astype(jnp.bfloat16)

    loop(tiles, own)
    for i in range(tensors - 1):
        peer = lax.rem(me + 1 + i, tensors)
        loop(tiles, lambda j, peer=peer: copy(peer, peer, j).wait_send())


def project_back(x, panel_rows, low, factor_cols, tensors):
    width, inner = panel_rows.shape
    rows = x.shape[0] // tensors
    tile = min(width, 512)
    tiles = width // tile
    vmem = pl.BlockSpec(memory_space=pltpu.VMEM)
    return pl.pallas_call(
        functools.partial(project_kernel, tensors),
        out_shape=jax.ShapeDtypeStruct((rows, width), jnp.bfloat16),
        in_specs=[vmem, pl.BlockSpec(memory_space=pl.ANY), vmem, vmem],
        out_specs=vmem,
        scratch_shapes=[
            pltpu.VMEM((width, inner), jnp.bfloat16),
            pltpu.VMEM((tensors, tiles, rows, tile), jnp.bfloat16),
            pltpu.VMEM((tensors, tiles, rows, tile), jnp.bfloat16),
            pltpu.SemaphoreType.DMA((tiles,)),
            pltpu.SemaphoreType.DMA((tensors, tiles)),
            pltpu.SemaphoreType.DMA((tensors, tiles)),
        ],
        compiler_params=pltpu.CompilerParams(
            collective_id=2, has_side_effects=True, vmem_limit_bytes=40 * 2**20
        ),
        cost_estimate=pl.CostEstimate(
            flops=2 * x.shape[0] * width * inner,
            bytes_accessed=2 * width * inner,
            transcendentals=0,
        ),
    )(x, panel_rows, low, factor_cols)


def body(
    layer_input,
    out_grad,
    ssd_output,
    gate_input,
    time_step,
    state_in,
    state_out,
    decay_rate,
    skip_gain,
    norm_gain,
    mixer_projection_weight,
    down_adapter_matrix,
    adapter_b,
):
    tensor_count = lax.axis_size("tensor")
    data_count = lax.axis_size("dp")
    seq_len = out_grad.shape[1]
    inner_dev = out_grad.shape[2]
    heads_dev = time_step.shape[2]
    head_size = inner_dev // heads_dev
    row_count = layer_input.shape[1]
    shard_rows = down_adapter_matrix.shape[0]
    inner_all = inner_dev * tensor_count
    grad_scale = float(data_count * seq_len) ** (-0.5)
    activation = jax.nn.silu(gate_input[0].astype(jnp.float32))
    gated_rows = ssd_output[0].astype(jnp.float32) * activation
    grad_rows = out_grad[0].astype(jnp.float32)
    gain_out = norm_gain.astype(jnp.float32)[None, :] * grad_rows
    sum_squares, cross_sum = lax.psum(
        jnp.stack(
            [jnp.sum(gated_rows * gated_rows, axis=1), jnp.sum(gain_out * gated_rows, axis=1)]
        ),
        "tensor",
    )
    inverse_rms = lax.rsqrt(sum_squares / inner_all + eps_norm)
    ssd_grad = (
        inverse_rms[:, None] * gain_out
        - gated_rows * (inverse_rms**3 * cross_sum / inner_all)[:, None]
    ) * activation
    gain_part = jnp.sum(grad_rows * gated_rows * inverse_rms[:, None], axis=0)
    scores = lax.dot_general(
        state_out[0], state_in[0], (((1,), (1,)), ((), ())), preferred_element_type=jnp.float32
    )
    cumulative = jnp.cumsum(-time_step[0] * decay_rate[None, :], axis=0)
    positions = jnp.arange(seq_len)
    causal = positions[:, None] >= positions[None, :]
    head_grads = jnp.transpose(
        ssd_grad.astype(jnp.bfloat16).reshape(seq_len, heads_dev, head_size), (1, 0, 2)
    )

    def per_head(head_items):
        head_cum, head_grad = head_items
        decay_gap = head_cum[:, None] - head_cum[None, :]
        mix_weights = (scores * jnp.exp(jnp.where(causal, decay_gap, -jnp.inf))).astype(
            jnp.bfloat16
        )
        return lax.dot_general(
            mix_weights, head_grad, (((0,), (0,)), ((), ())), preferred_element_type=jnp.float32
        )

    state_back = lax.map(per_head, (cumulative.T, head_grads))
    mixer_input_gradient = (
        (
            time_step[0][:, :, None] * jnp.transpose(state_back, (1, 0, 2))
            + skip_gain[None, :, None] * ssd_grad.reshape(seq_len, heads_dev, head_size)
        )
        .reshape(seq_len, inner_dev)
        .astype(jnp.bfloat16)
    )
    adapter_portion = lax.dot_general(
        mixer_input_gradient,
        adapter_b,
        (((1,), (1,)), ((), ())),
        preferred_element_type=jnp.float32,
    )
    adapter_total = lax.psum(adapter_portion, "tensor")
    own_rows = lax.dynamic_slice_in_dim(
        adapter_total, lax.axis_index("tensor") * row_count, row_count, 0
    ).astype(jnp.bfloat16)
    adapter_bf = adapter_portion.astype(jnp.bfloat16)
    sequence_input = layer_input[0]
    rank = down_adapter_matrix.shape[1]
    panel_rows = lax.all_gather(mixer_projection_weight, "dp", axis=0, tiled=True)
    factor_cols = (
        gather_rows(down_adapter_matrix.T, data_count).transpose(1, 0, 2).reshape(rank, -1)
    )
    first_factor_partial = low_rank_scale * lax.dot_general(
        own_rows, sequence_input, (((0,), (0,)), ((), ())), preferred_element_type=jnp.float32
    )
    a_parts = first_factor_partial.reshape(rank, data_count, shard_rows).transpose(1, 0, 2)
    adapter_input_rows = lax.dot_general(
        sequence_input, factor_cols, (((1,), (1,)), ((), ())), preferred_element_type=jnp.float32
    )
    adapter_full = lax.all_gather(
        adapter_input_rows.astype(jnp.bfloat16), "tensor", axis=0, tiled=True
    )
    second_factor_partial = low_rank_scale * lax.dot_general(
        adapter_full,
        mixer_input_gradient,
        (((0,), (0,)), ((), ())),
        preferred_element_type=jnp.float32,
    )
    b_words = (rank + 1) * inner_dev
    chunk_rows = -(-b_words // (data_count * 2048)) * 16
    b_parts = jnp.concatenate(
        [
            second_factor_partial.reshape(-1, 128),
            gain_part.reshape(-1, 128),
            jnp.zeros((data_count * chunk_rows - b_words // 128, 128), jnp.float32),
        ]
    ).reshape(data_count, chunk_rows, 128)
    a_total, b_total = reduce_all(
        a_parts.astype(jnp.bfloat16), b_parts.astype(jnp.bfloat16), tensor_count, grad_scale
    )
    panel_rows, a_total, b_total = lax.optimization_barrier((panel_rows, a_total, b_total))
    b_lines = b_total.reshape(-1, 128)
    b_count = rank * inner_dev // 128
    adapter_b_grad = b_lines[:b_count].reshape(rank, inner_dev)
    gain_grad = b_lines[b_count : b_words // 128].reshape(inner_dev)
    input_grad = project_back(
        mixer_input_gradient, panel_rows, adapter_bf, factor_cols, tensor_count
    )[None]
    return (input_grad, a_total.T, adapter_b_grad, gain_grad)


def solution(mesh):
    return jax.shard_map(
        body,
        mesh=mesh,
        in_specs=(
            P("dp", "tensor", None),
            P("dp", None, "tensor"),
            P("dp", None, "tensor"),
            P("dp", None, "tensor"),
            P("dp", None, "tensor"),
            P("dp", None, "tensor"),
            P("dp", None, "tensor"),
            P("tensor"),
            P("tensor"),
            P("tensor"),
            P("dp", "tensor"),
            P("dp", None),
            P(None, "tensor"),
        ),
        out_specs=(P("dp", "tensor", None), P("dp", None), P(None, "tensor"), P("tensor")),
        check_vma=False,
    )
```

```python
import functools

import jax
import jax.numpy as jnp
from jax import lax
from jax.experimental import pallas as pl
from jax.experimental.pallas import tpu as pltpu
from jax.sharding import PartitionSpec as P

eps_norm = 1e-05
low_rank_scale = 2.0
MESH = pl.DeviceIdType.MESH


def loop(count, step):
    def run(i, carry):
        step(i)
        return carry

    lax.fori_loop(0, count, run, 0)


def greet_kernel_peers(axis_counts):
    barrier = pltpu.get_barrier_semaphore()
    for axis, count in axis_counts:
        me = lax.axis_index(axis)
        loop(
            count - 1,
            lambda i, axis=axis, me=me, count=count: pl.semaphore_signal(
                barrier, inc=1, device_id={axis: lax.rem(me + 1 + i, count)}, device_id_type=MESH
            ),
        )
    pl.semaphore_wait(barrier, sum(count - 1 for _, count in axis_counts))


def exchange(axis, count, source, landing, send_sem, recv_sem):
    me = lax.axis_index(axis)

    def copy(peer, slot):
        return pltpu.make_async_remote_copy(
            src_ref=source(peer),
            dst_ref=landing.at[slot],
            send_sem=send_sem.at[peer],
            recv_sem=recv_sem.at[slot],
            device_id={axis: peer},
            device_id_type=MESH,
        )

    def start(i):
        copy(lax.rem(me + 1 + i, count), me).start()

    def finish(i):
        peer = lax.rem(me + 1 + i, count)
        copy(peer, peer).wait_send()
        copy(peer, peer).wait_recv()

    return lambda: loop(count - 1, start), lambda: loop(count - 1, finish)


def gather_kernel(count, own_ref, out_ref, landing, send_sem, recv_sem):
    me = lax.axis_index("dp")
    greet_kernel_peers((("dp", count),))
    start, finish = exchange("dp", count, lambda peer: own_ref, landing, send_sem, recv_sem)
    start()
    landing[me] = own_ref[...]
    finish()
    out_ref[...] = landing[...]


def gather_rows(own, count):
    shape = (count,) + own.shape
    return pl.pallas_call(
        functools.partial(gather_kernel, count),
        out_shape=jax.ShapeDtypeStruct(shape, own.dtype),
        in_specs=[pl.BlockSpec(memory_space=pltpu.VMEM)],
        out_specs=pl.BlockSpec(memory_space=pltpu.VMEM),
        scratch_shapes=[
            pltpu.VMEM(shape, own.dtype),
            pltpu.SemaphoreType.DMA((count,)),
            pltpu.SemaphoreType.DMA((count,)),
        ],
        compiler_params=pltpu.CompilerParams(
            collective_id=0, has_side_effects=True, vmem_limit_bytes=16 * 2**20
        ),
    )(own)


def reduce_kernel(
    count, tensors, scale, a_ref, b_ref, a_out, b_out,
    a_land, b_land, a_pair, b_back, a_part, b_part,
    a_send, a_recv, b_send, b_recv, p_send, p_recv, r_send, r_recv,
):
    me = lax.axis_index("dp")
    pair_me = lax.axis_index("tensor")
    greet_kernel_peers((("dp", count), ("tensor", tensors)))
    b_start, b_finish = exchange("dp", count, lambda p: b_ref.at[p], b_land, b_send, b_recv)
    a_start, a_finish = exchange("dp", count, lambda p: a_ref.at[p], a_land, a_send, a_recv)
    r_start, r_finish = exchange("dp", count, lambda p: b_part, b_back, r_send, r_recv)
    p_start, p_finish = exchange("tensor", tensors, lambda p: a_part, a_pair, p_send, p_recv)
    b_start()
    a_start()

    b_part[...] = b_ref[me].astype(jnp.float32)
    a_part[...] = a_ref[me].astype(jnp.float32)
    b_finish()

    def add_b(i):
        b_part[...] += b_land[lax.rem(me + 1 + i, count)].astype(jnp.float32)

    loop(count - 1, add_b)
    b_part[...] *= scale
    r_start()
    b_back[me] = b_part[...]
    a_finish()

    def add_a(i):
        a_part[...] += a_land[lax.rem(me + 1 + i, count)].astype(jnp.float32)

    loop(count - 1, add_a)
    p_start()
    a_pair[pair_me] = a_part[...]
    p_finish()
    total = a_pair[0]
    for k in range(1, tensors):
        total = total + a_pair[k]
    a_out[...] = total * scale
    r_finish()
    b_out[...] = b_back[...]


def reduce_all(a_parts, b_parts, tensors, scale):
    count = a_parts.shape[0]
    f32 = jnp.float32
    return pl.pallas_call(
        functools.partial(reduce_kernel, count, tensors, scale),
        out_shape=(
            jax.ShapeDtypeStruct(a_parts.shape[1:], f32),
            jax.ShapeDtypeStruct(b_parts.shape, f32),
        ),
        in_specs=[pl.BlockSpec(memory_space=pltpu.VMEM)] * 2,
        out_specs=(pl.BlockSpec(memory_space=pltpu.VMEM),) * 2,
        scratch_shapes=[
            pltpu.VMEM(a_parts.shape, a_parts.dtype),
            pltpu.VMEM(b_parts.shape, b_parts.dtype),
            pltpu.VMEM((tensors,) + a_parts.shape[1:], f32),
            pltpu.VMEM(b_parts.shape, f32),
            pltpu.VMEM(a_parts.shape[1:], f32),
            pltpu.VMEM(b_parts.shape[1:], f32),
        ]
        + [pltpu.SemaphoreType.DMA((count,))] * 4
        + [pltpu.SemaphoreType.DMA((tensors,))] * 2
        + [pltpu.SemaphoreType.DMA((count,))] * 2,
        compiler_params=pltpu.CompilerParams(
            collective_id=1, has_side_effects=True, vmem_limit_bytes=16 * 2**20
        ),
    )(a_parts, b_parts)


def project_kernel(
    tensors, x_ref, panel_hbm, low_ref, factor_ref, out_ref,
    panel, outgoing, landing, panel_sem, send_sem, recv_sem,
):
    me = lax.axis_index("tensor")
    rows = out_ref.shape[0]
    _, tiles, _, tile = landing.shape

    def columns(j):
        return pl.ds(pl.multiple_of(j * tile, tile), tile)

    def fetch(j):
        return pltpu.make_async_copy(
            panel_hbm.at[columns(j)], panel.at[columns(j)], panel_sem.at[j]
        )

    def copy(peer, slot, j):
        return pltpu.make_async_remote_copy(
            src_ref=outgoing.at[peer, j],
            dst_ref=landing.at[slot, j],
            send_sem=send_sem.at[peer, j],
            recv_sem=recv_sem.at[slot, j],
            device_id={"tensor": peer},
            device_id_type=MESH,
        )

    def product(owner, j):
        tokens = pl.ds(pl.multiple_of(owner * rows, rows), rows)
        full = lax.dot_general(
            x_ref[tokens, :], panel[columns(j), :], (((1,), (1,)), ((), ())),
            preferred_element_type=jnp.float32,
        )
        low = jnp.dot(
            low_ref[tokens, :], factor_ref[:, columns(j)], preferred_element_type=jnp.float32
        )
        return (full + low_rank_scale * low).astype(jnp.bfloat16)

    loop(tiles, lambda j: fetch(j).start())
    greet_kernel_peers((("tensor", tensors),))
    for i in range(tensors - 1):
        peer = lax.rem(me + 1 + i, tensors)

        def send(j, i=i, peer=peer):
            if i == 0:
                fetch(j).wait()
            outgoing[peer, j] = product(peer, j)
            copy(peer, me, j).start()

        loop(tiles, send)

    def own(j):
        total = product(me, j).astype(jnp.float32)
        for i in range(tensors - 1):
            peer = lax.rem(me + 1 + i, tensors)
            copy(peer, peer, j).wait_recv()
            total = total + landing[peer, j].astype(jnp.float32)
        out_ref[:, columns(j)] = total.astype(jnp.bfloat16)

    loop(tiles, own)
    for i in range(tensors - 1):
        peer = lax.rem(me + 1 + i, tensors)
        loop(tiles, lambda j, peer=peer: copy(peer, peer, j).wait_send())


def project_back(x, panel_rows, low, factor_cols, tensors):
    width, inner = panel_rows.shape
    rows = x.shape[0] // tensors
    tile = min(width, 512)
    tiles = width // tile
    vmem = pl.BlockSpec(memory_space=pltpu.VMEM)
    return pl.pallas_call(
        functools.partial(project_kernel, tensors),
        out_shape=jax.ShapeDtypeStruct((rows, width), jnp.bfloat16),
        in_specs=[vmem, pl.BlockSpec(memory_space=pltpu.HBM), vmem, vmem],
        out_specs=vmem,
        scratch_shapes=[
            pltpu.VMEM((width, inner), jnp.bfloat16),
            pltpu.VMEM((tensors, tiles, rows, tile), jnp.bfloat16),
            pltpu.VMEM((tensors, tiles, rows, tile), jnp.bfloat16),
            pltpu.SemaphoreType.DMA((tiles,)),
            pltpu.SemaphoreType.DMA((tensors, tiles)),
            pltpu.SemaphoreType.DMA((tensors, tiles)),
        ],
        compiler_params=pltpu.CompilerParams(
            collective_id=2, has_side_effects=True, vmem_limit_bytes=40 * 2**20
        ),
        cost_estimate=pl.CostEstimate(
            flops=2 * x.shape[0] * width * inner,
            bytes_accessed=2 * width * inner,
            transcendentals=0,
        ),
    )(x, panel_rows, low, factor_cols)


def body(
    layer_input,
    out_grad,
    ssd_output,
    gate_input,
    time_step,
    state_in,
    state_out,
    decay_rate,
    skip_gain,
    norm_gain,
    mixer_projection_weight,
    down_adapter_matrix,
    adapter_b,
):
    tensor_count = lax.axis_size("tensor")
    data_count = lax.axis_size("dp")
    seq_len = out_grad.shape[1]
    inner_dev = out_grad.shape[2]
    heads_dev = time_step.shape[2]
    head_size = inner_dev // heads_dev
    row_count = layer_input.shape[1]
    shard_rows = down_adapter_matrix.shape[0]
    inner_all = inner_dev * tensor_count
    grad_scale = float(data_count * seq_len) ** (-0.5)
    activation = jax.nn.silu(gate_input[0].astype(jnp.float32))
    gated_rows = ssd_output[0].astype(jnp.float32) * activation
    grad_rows = out_grad[0].astype(jnp.float32)
    gain_out = norm_gain.astype(jnp.float32)[None, :] * grad_rows
    sum_squares, cross_sum = lax.psum(
        jnp.stack(
            [jnp.sum(gated_rows * gated_rows, axis=1), jnp.sum(gain_out * gated_rows, axis=1)]
        ),
        "tensor",
    )
    inverse_rms = lax.rsqrt(sum_squares / inner_all + eps_norm)
    ssd_grad = (
        inverse_rms[:, None] * gain_out
        - gated_rows * (inverse_rms**3 * cross_sum / inner_all)[:, None]
    ) * activation
    gain_part = jnp.sum(grad_rows * gated_rows * inverse_rms[:, None], axis=0)
    scores = lax.dot_general(
        state_out[0], state_in[0], (((1,), (1,)), ((), ())), preferred_element_type=jnp.float32
    )
    cumulative = jnp.cumsum(-time_step[0] * decay_rate[None, :], axis=0)
    positions = jnp.arange(seq_len)
    causal = positions[:, None] >= positions[None, :]
    head_grads = jnp.transpose(
        ssd_grad.astype(jnp.bfloat16).reshape(seq_len, heads_dev, head_size), (1, 0, 2)
    )

    def per_head(head_items):
        head_cum, head_grad = head_items
        decay_gap = head_cum[:, None] - head_cum[None, :]
        mix_weights = (scores * jnp.exp(jnp.where(causal, decay_gap, -jnp.inf))).astype(
            jnp.bfloat16
        )
        return lax.dot_general(
            mix_weights, head_grad, (((0,), (0,)), ((), ())), preferred_element_type=jnp.float32
        )

    state_back = lax.map(per_head, (cumulative.T, head_grads))
    mixer_input_gradient = (
        (
            time_step[0][:, :, None] * jnp.transpose(state_back, (1, 0, 2))
            + skip_gain[None, :, None] * ssd_grad.reshape(seq_len, heads_dev, head_size)
        )
        .reshape(seq_len, inner_dev)
        .astype(jnp.bfloat16)
    )
    adapter_portion = lax.dot_general(
        mixer_input_gradient,
        adapter_b,
        (((1,), (1,)), ((), ())),
        preferred_element_type=jnp.float32,
    )
    adapter_total = lax.psum(adapter_portion, "tensor")
    own_rows = lax.dynamic_slice_in_dim(
        adapter_total, lax.axis_index("tensor") * row_count, row_count, 0
    ).astype(jnp.bfloat16)
    adapter_bf = adapter_portion.astype(jnp.bfloat16)
    sequence_input = layer_input[0]
    rank = down_adapter_matrix.shape[1]
    panel_rows = lax.all_gather(mixer_projection_weight, "dp", axis=0, tiled=True)
    factor_cols = (
        gather_rows(down_adapter_matrix.T, data_count).transpose(1, 0, 2).reshape(rank, -1)
    )
    first_factor_partial = low_rank_scale * lax.dot_general(
        own_rows, sequence_input, (((0,), (0,)), ((), ())), preferred_element_type=jnp.float32
    )
    a_parts = first_factor_partial.reshape(rank, data_count, shard_rows).transpose(1, 0, 2)
    adapter_input_rows = lax.dot_general(
        sequence_input, factor_cols, (((1,), (1,)), ((), ())), preferred_element_type=jnp.float32
    )
    adapter_full = lax.all_gather(
        adapter_input_rows.astype(jnp.bfloat16), "tensor", axis=0, tiled=True
    )
    second_factor_partial = low_rank_scale * lax.dot_general(
        adapter_full,
        mixer_input_gradient,
        (((0,), (0,)), ((), ())),
        preferred_element_type=jnp.float32,
    )
    b_words = (rank + 1) * inner_dev
    chunk_rows = -(-b_words // (data_count * 2048)) * 16
    b_parts = jnp.concatenate(
        [
            second_factor_partial.reshape(-1, 128),
            gain_part.reshape(-1, 128),
            jnp.zeros((data_count * chunk_rows - b_words // 128, 128), jnp.float32),
        ]
    ).reshape(data_count, chunk_rows, 128)
    a_total, b_total = reduce_all(
        a_parts.astype(jnp.bfloat16), b_parts.astype(jnp.bfloat16), tensor_count, grad_scale
    )
    b_lines = b_total.reshape(-1, 128)
    b_count = rank * inner_dev // 128
    adapter_b_grad = b_lines[:b_count].reshape(rank, inner_dev)
    gain_grad = b_lines[b_count : b_words // 128].reshape(inner_dev)
    panel_rows, adapter_a_grad, adapter_b_grad, gain_grad = lax.optimization_barrier(
        (panel_rows, a_total.T, adapter_b_grad, gain_grad)
    )
    input_grad = project_back(
        mixer_input_gradient, panel_rows, adapter_bf, factor_cols, tensor_count
    )[None]
    return (input_grad, adapter_a_grad, adapter_b_grad, gain_grad)


def solution(mesh):
    return jax.shard_map(
        body,
        mesh=mesh,
        in_specs=(
            P("dp", "tensor", None),
            P("dp", None, "tensor"),
            P("dp", None, "tensor"),
            P("dp", None, "tensor"),
            P("dp", None, "tensor"),
            P("dp", None, "tensor"),
            P("dp", None, "tensor"),
            P("tensor"),
            P("tensor"),
            P("tensor"),
            P("dp", "tensor"),
            P("dp", None),
            P(None, "tensor"),
        ),
        out_specs=(P("dp", "tensor", None), P("dp", None), P(None, "tensor"), P("tensor")),
        check_vma=False,
    )
```
